32 devices in a mesh: groups: 2 (over x), seq: 4 (over y, core), dp: 4 (over z).
Axes of the slice: x: 2, y: 2, z: 4, core: 2. Of those that a mesh axis runs over, the one named last changes fastest.
Arguments:
- stream_in: bfloat16 [8, 2048, 512], P(('groups', 'dp'), 'seq'), parts along dimension 0, may hold values from -6 to 6
- conv_weight: bfloat16 [2, 1536, 1024], replicated, may hold values from -0.15625 to 0.15625
- res_weight: bfloat16 [2, 512, 512], replicated, may hold values from -0.25 to 0.25
- out_cotangent: bfloat16 [8, 2048, 512], P(('groups', 'dp'), 'seq'), parts along dimension 0, may hold values from -6 to 6
Outputs:
- output: bfloat16 [8, 2048, 512], P(('groups', 'dp'), 'seq'), parts along dimension 0
- input_grad: float32 [8, 2048, 512], P(('groups', 'dp'), 'seq'), parts along dimension 0
- grad_conv: float32 [4, 1536, 1024], P('groups', 'seq', 'dp'), parts along dimension 0
- grad_res: float32 [4, 512, 512], P('groups', 'seq', 'dp'), parts along dimension 0
The draws below stay inside these ranges and needn't reach their ends.
There are 2 independent parts, one for each index of `groups`. The reference program is written for one: setup_inputs(seed, part) draws one part's arguments, and reference() takes and returns one part's arrays. A program takes and returns all parts, laid end to end along the dimension named above; an argument that names none is the same for every part. Nothing has to cross between parts.
All inputs are finite; a program needn't handle non-finite values.
Results may differ from the reference program's by a relative error of at most 0.0055.
Values may be sent and summed in bfloat16 or wider, within the bound.
A program may use at most 128 MiB of HBM per device.

```python
import jax
import jax.numpy as jnp

C = 512
LAYERS = 2
DILATION = 512
LEN = 2048
RECORDS = 4


def with_spikes(drawn, rng, source, target, shards_of, factor):
    owner, partner = [(jnp.arange(drawn.shape[position]) // (drawn.shape[position] // shards_of)).reshape([-1 if axis == position else 1 for axis in range(drawn.ndim)]) for position in (source, target)]
    chosen = jax.random.permutation(rng, shards_of)[partner]
    strong = (owner == chosen) | (owner == (partner + shards_of // 2) % shards_of)
    return jnp.where(strong, factor * drawn, drawn)


def steps_of(rng, extent, split, low, high):
    def one(dim, parts):
        draws = jax.random.uniform(jax.random.fold_in(jax.random.fold_in(rng, 6), dim), (parts,), jnp.float32, low / len(split), high / len(split))
        return jnp.repeat(jnp.exp(draws), extent[dim] // parts).reshape((-1,) + (1,) * (len(extent) - dim - 1))

    factor_of = one(*split[0])
    for cut in split[1:]:
        factor_of = factor_of * one(*cut)
    return factor_of


def centred(key, extent, scale, limit, cuts=(), dtype=jnp.bfloat16):
    drawn = jax.random.normal(key, extent, jnp.float32) * scale
    if len(cuts) > 0:
        drawn = steps_of(key, extent, cuts, -0.22, 0.18) * drawn
    return jnp.clip(drawn, min=-limit, max=limit).astype(dtype)


def bell_draw_with(stream_key, shape, scale, limit, split, heavy, dtype=jnp.bfloat16):
    array = scale * jax.random.normal(stream_key, shape, jnp.float32)
    if split:
        array = array * steps_of(stream_key, shape, split, -0.22, 0.18)
    return jnp.clip(with_spikes(array, jax.random.fold_in(stream_key, 3), *heavy), -limit, limit).astype(dtype)


def setup_inputs(seed: int = 0, part: int = 0) -> dict:
    keys = jax.random.split(jax.random.key(seed), 5)
    part_keys = jax.random.split(jax.random.fold_in(keys[4], part), 5)
    stream_in = bell_draw_with(part_keys[0], (RECORDS, LEN, C), 1.0, 6.0, ((0, 4), (1, 4)), (1, 2, 4, 2.0))
    conv_weight = centred(keys[1], (LAYERS, 3 * C, 2 * C), (3 * C) ** -0.5, 0.15625)
    res_weight = centred(keys[2], (LAYERS, C, C), C ** -0.5, 0.25)
    out_cotangent = centred(part_keys[3], (RECORDS, LEN, C), 1.0, 6.0, ((0, 4), (1, 4)))
    return dict(stream_in=stream_in, conv_weight=conv_weight, res_weight=res_weight, out_cotangent=out_cotangent)


def delayed(values, offset):
    total = values.shape[1]
    if offset >= total:
        return jnp.zeros_like(values)
    padded = jnp.pad(values, ((0, 0), (offset, 0), (0, 0)))
    return padded[:, :total]


def advanced(values, offset):
    total = values.shape[1]
    if offset >= total:
        return jnp.zeros_like(values)
    padded = jnp.pad(values, ((0, 0), (0, offset), (0, 0)))
    return padded[:, offset:offset + total]


def reference(stream_in, conv_weight, res_weight, out_cotangent):
    records, length, channels = stream_in.shape
    stream = stream_in
    stored = []
    for layer_index in range(LAYERS):
        spacing = DILATION * 4 ** layer_index
        taps = jnp.concatenate([stream, delayed(stream, spacing), delayed(stream, 2 * spacing)], axis=2)
        taps_flat = taps.reshape(records * length, 3 * channels)
        preact = jnp.dot(taps_flat, conv_weight[layer_index], preferred_element_type=jnp.float32)
        filter_value = jnp.tanh(preact[:, :channels])
        gate_value = jax.nn.sigmoid(preact[:, channels:])
        gated = (filter_value * gate_value).astype(jnp.bfloat16)
        update = jnp.dot(gated, res_weight[layer_index], preferred_element_type=jnp.float32)
        stream = (stream.reshape(-1, channels).astype(jnp.float32) + update).astype(jnp.bfloat16).reshape(records, length, channels)
        stored.append((taps_flat, filter_value, gate_value, gated))
    stream_grad = out_cotangent.astype(jnp.float32).reshape(-1, channels)
    conv_grads = [None] * LAYERS
    res_grads = [None] * LAYERS
    for layer_index in reversed(range(LAYERS)):
        spacing = DILATION * 4 ** layer_index
        taps_flat, filter_value, gate_value, gated = stored[layer_index]
        signal = stream_grad.astype(jnp.bfloat16)
        res_grads[layer_index] = jnp.dot(gated.T, signal, preferred_element_type=jnp.float32)
        gated_grad = jnp.dot(signal, res_weight[layer_index].T, preferred_element_type=jnp.float32)
        filter_grad = gated_grad * gate_value * (1.0 - filter_value * filter_value)
        gate_grad = gated_grad * filter_value * gate_value * (1.0 - gate_value)
        pre_grad = jnp.concatenate([filter_grad, gate_grad], axis=1).astype(jnp.bfloat16)
        conv_grads[layer_index] = jnp.dot(taps_flat.T, pre_grad, preferred_element_type=jnp.float32)
        tap_grads = jnp.dot(pre_grad, conv_weight[layer_index].T, preferred_element_type=jnp.float32).astype(jnp.bfloat16)
        tap_grads = tap_grads.reshape(records, length, 3 * channels)
        first = tap_grads[:, :, :channels].astype(jnp.float32)
        second = advanced(tap_grads[:, :, channels:2 * channels], spacing).astype(jnp.float32)
        third = advanced(tap_grads[:, :, 2 * channels:], 2 * spacing).astype(jnp.float32)
        stream_grad = stream_grad + (first + second + third).reshape(-1, channels)
    input_grad = stream_grad.reshape(records, length, channels)
    return stream, input_grad, jnp.stack(conv_grads), jnp.stack(res_grads)
```

```python
import functools

import jax
import jax.numpy as jnp
from jax import lax
from jax.experimental import pallas as pl
from jax.experimental.pallas import tpu as pltpu
from jax.sharding import PartitionSpec as P

DILATION = 512


def shifted(value, axis, steps):
    count = lax.axis_size(axis)
    leading, last = (max(0, -steps), min(count, count - steps))
    return lax.ppermute(value, axis, [(source, source + steps) for source in range(leading, last)])


def moved_back(values, distance):
    if distance >= lax.axis_size("seq"):
        return jnp.zeros_like(values)
    return shifted(values, "seq", distance)


def moved_ahead(values, distance):
    if distance >= lax.axis_size("seq"):
        return jnp.zeros_like(values)
    return shifted(values, "seq", -distance)


def looking_back(values, offset):
    length = values.shape[1]
    whole_shards, remainder = divmod(offset, length)
    return moved_back(values, whole_shards)


def looking_ahead(values, offset):
    length = values.shape[1]
    whole_shards, remainder = divmod(offset, length)
    return moved_ahead(values, whole_shards)


def spread_sum(left_side, right_side):
    contract = (((0,), (0,)), ((), ()))
    partial_value = lax.psum_scatter(
        lax.dot_general(left_side, right_side, contract, preferred_element_type=jnp.float32),
        "seq",
        scatter_dimension=0,
        tiled=True,
    )
    return lax.psum_scatter(partial_value, "dp", scatter_dimension=1, tiled=True)


def local(stream_in, conv_weight, res_weight, out_cotangent):
    records, length, channels = stream_in.shape
    layer_count = conv_weight.shape[0]
    stream = stream_in
    stored = []
    for layer_index in range(layer_count):
        spacing = DILATION * 4**layer_index
        taps = jnp.concatenate(
            [stream, looking_back(stream, spacing), looking_back(stream, 2 * spacing)], axis=2
        )
        taps_flat = taps.reshape(records * length, 3 * channels)
        preact = jnp.dot(taps_flat, conv_weight[layer_index], preferred_element_type=jnp.float32)
        filter_value = jnp.tanh(preact[:, :channels])
        gate_value = jax.nn.sigmoid(preact[:, channels:])
        gated = (filter_value * gate_value).astype(jnp.bfloat16)
        update = jnp.dot(gated, res_weight[layer_index], preferred_element_type=jnp.float32)
        stream = (
            (stream.reshape(-1, channels).astype(jnp.float32) + update)
            .astype(jnp.bfloat16)
            .reshape(records, length, channels)
        )
        stored.append((taps_flat, filter_value, gate_value, gated))
    stream_grad = out_cotangent.astype(jnp.float32).reshape(-1, channels)
    transpose_rhs = (((1,), (1,)), ((), ()))
    conv_grads = [None] * layer_count
    res_grads = [None] * layer_count
    for layer_index in reversed(range(layer_count)):
        spacing = DILATION * 4**layer_index
        taps_flat, filter_value, gate_value, gated = stored[layer_index]
        signal = stream_grad.astype(jnp.bfloat16)
        res_grads[layer_index] = spread_sum(gated, signal)
        gated_grad = lax.dot_general(
            signal, res_weight[layer_index], transpose_rhs, preferred_element_type=jnp.float32
        )
        filter_grad = gated_grad * gate_value * (1.0 - filter_value * filter_value)
        gate_grad = gated_grad * filter_value * gate_value * (1.0 - gate_value)
        pre_grad = jnp.concatenate([filter_grad, gate_grad], axis=1).astype(jnp.bfloat16)
        conv_grads[layer_index] = spread_sum(taps_flat, pre_grad)
        tap_grads = lax.dot_general(
            pre_grad, conv_weight[layer_index], transpose_rhs, preferred_element_type=jnp.float32
        ).astype(jnp.bfloat16)
        tap_grads = tap_grads.reshape(records, length, 3 * channels)
        first = tap_grads[:, :, :channels].astype(jnp.float32)
        second = looking_ahead(tap_grads[:, :, channels : 2 * channels], spacing).astype(
            jnp.float32
        )
        third = looking_ahead(tap_grads[:, :, 2 * channels :], 2 * spacing).astype(jnp.float32)
        stream_grad = stream_grad + (first + second + third).reshape(-1, channels)
    input_grad = stream_grad.reshape(records, length, channels)
    return (stream, input_grad, jnp.stack(conv_grads), jnp.stack(res_grads))


BF16 = jnp.bfloat16
F32 = jnp.float32
MESH = pl.DeviceIdType.MESH


def mm(left, right):
    return jnp.dot(left, right, preferred_element_type=F32)


def mm_nt(left, right):
    return lax.dot_general(left, right, (((1,), (1,)), ((), ())), preferred_element_type=F32)


def mm_tn(left, right):
    return lax.dot_general(left, right, (((0,), (0,)), ((), ())), preferred_element_type=F32)


def fused_kernel(
    dp_count,
    x_ref, w_ref, r_ref, ct_ref,
    out_ref, ig_ref, gc_ref, gr_ref,
    sbuf, w0, w1, rw, ctb,
    fa0, fb0, fa1, fb1, z0, z1, s1, dpre, g1, lt,
    outv, igv, hsend, hrecv,
    acc0, acc1, accr,
    cs0, cr0, cs1, cr1, csr, crr,
    zs0, zr0, zs1, zr1, zsr, zrr,
    fs1, fr1, gcv, grv,
    lsem, osem, ys_s, ys_r, yc_s, yc_r, xs_s, xs_r, fw_s, fw_r, h_s, h_r,
    c0_s, c0_r, c1_s, c1_r, cr_s, cr_r,
    za_s, za_r, zb_s, zb_r, zc_s, zc_r, f_s, f_r,
):
    s = lax.axis_index("seq")
    p = lax.axis_index("dp")
    y = s // 2
    c = s % 2
    other = s + 1 - 2 * c
    across = s + 2 - 4 * y
    length, chan = x_ref.shape[1], x_ref.shape[2]
    half = length // 2
    width = 2 * chan
    col = width // dp_count
    rcol = chan // dp_count
    own0 = 3 * chan // 4
    own1 = chan // 4
    ymid = pl.multiple_of(y * (chan // 2), 256)

    local_copies = [
        pltpu.make_async_copy(x_ref.at[0], sbuf.at[2 + s], lsem.at[0]),
        pltpu.make_async_copy(w_ref.at[0], w0, lsem.at[1]),
        pltpu.make_async_copy(r_ref, rw, lsem.at[2]),
        pltpu.make_async_copy(w_ref.at[1, pl.ds(0, chan)], w1, lsem.at[3]),
        pltpu.make_async_copy(ct_ref.at[0], ctb.at[0], lsem.at[4]),
    ]
    for copy in local_copies:
        copy.start()

    barrier = pltpu.get_barrier_semaphore()
    peers = [{"seq": other}, {"seq": across}]
    peers += [{"dp": (p + k) % dp_count} for k in range(1, dp_count)]
    for peer in peers:
        pl.semaphore_signal(barrier, inc=1, device_id=peer, device_id_type=MESH)
    pl.semaphore_wait(barrier, len(peers))

    def remote(src, dst, send, recv, device):
        return pltpu.make_async_remote_copy(
            src_ref=src, dst_ref=dst, send_sem=send, recv_sem=recv,
            device_id=device, device_id_type=MESH,
        )

    def rows(h):
        return pl.ds(h * half, half)

    s_over = [
        remote(x_ref.at[0, rows(h)], sbuf.at[2 + s, rows(h)], ys_s.at[h], ys_r.at[h], {"seq": across})
        for h in range(2)
    ]
    c_over = [
        remote(ct_ref.at[0, rows(h)], ctb.at[1, rows(h)], yc_s.at[h], yc_r.at[h], {"seq": across})
        for h in range(2)
    ]
    s_pair = remote(x_ref.at[0], sbuf.at[2 + s], xs_s, xs_r, {"seq": other})
    s_fwd = [
        remote(sbuf.at[2 + across, rows(h)], sbuf.at[2 + across, rows(h)], fw_s.at[h], fw_r.at[h],
               {"seq": other})
        for h in range(2)
    ]
    for h in range(2):
        s_over[h].start()
    s_pair.start()
    for h in range(2):
        c_over[h].start()

    sbuf[pl.ds(0, 2)] = jnp.zeros((2, length, chan), BF16)

    @pl.when(c == 0)
    def _():
        hsend[...] = jnp.zeros_like(hsend)

    for copy in local_copies:
        copy.wait()
    s_pair.wait_recv()

    def take_over():
        for h in range(2):
            s_over[h].wait_recv()
            s_fwd[h].start()
        for h in range(2):
            s_fwd[h].wait_recv()

    pl.when(y == 1)(take_over)

    def forward(k, u):
        def part(h, _):
            r = pl.ds(pl.multiple_of(h * half, half), half)
            now, back, back2 = sbuf[u + 2, r], sbuf[u + 1, r], sbuf[u, r]

            def pre(lo):
                return (
                    mm(now, w0[0:chan, lo : lo + chan])
                    + mm(back, w0[chan : 2 * chan, lo : lo + chan])
                    + mm(back2, w0[2 * chan :, lo : lo + chan])
                )

            def gate(filt, sig, fa, fb):
                f = jnp.tanh(filt)
                g = 0.5 * jnp.tanh(0.5 * sig) + 0.5
                fa[r] = g * (1.0 - f * f)
                fg = f * g
                fb[r] = fg * (1.0 - g)
                return fg.astype(BF16)

            z = gate(pre(0), pre(chan), fa0, fb0)
            z0[r] = z
            nxt = (now.astype(F32) + mm(z, rw[0])).astype(BF16)
            s1[r] = nxt
            z = gate(mm(nxt, w1[:, 0:chan]), mm(nxt, w1[:, chan:]), fa1, fb1)
            z1[r] = z
            if k == 0:
                outv[r] = (nxt.astype(F32) + mm(z, rw[1])).astype(BF16)
            return 0

        lax.fori_loop(0, 2, part, 0)

    def transposed(u):
        lt[pl.ds(ymid, chan)] = sbuf[u + 2 * (1 - y)].T
        small = sbuf[u + 1, :, pl.ds(ymid, chan // 2)]
        lt[pl.ds(pl.multiple_of((1 - y) * chan, 256), chan // 2)] = small.T

    def back_one(k, u):
        def part(h, _):
            r = pl.ds(pl.multiple_of(h * half, half), half)
            if k == 1:
                for hh in range(2):
                    @pl.when(h == hh)
                    def _():
                        c_over[hh].wait_recv()
            e = ctb[k, r]
            dz = mm_nt(e, rw[1])
            df = (dz * fa1[r]).astype(BF16)
            dg = (dz * fb1[r]).astype(BF16)
            dpre[r, 0:chan] = df
            dpre[r, chan:] = dg
            g1[r] = e.astype(F32) + mm_nt(df, w1[:, 0:chan]) + mm_nt(dg, w1[:, chan:])
            return 0

        lax.fori_loop(0, 2, part, 0)
        gr1 = mm_tn(z1[:, pl.ds(ymid, chan // 2)], ctb[k])
        gc1 = mm_tn(s1[:, pl.ds(ymid, chan // 2)], dpre[...])
        if k == 0:
            accr[1] = gr1
            acc1[...] = gc1
        else:
            accr[1] = accr[1] + gr1
            acc1[...] = acc1[...] + gc1

    def back_zero(k, u):
        def part(h, _):
            r = pl.ds(pl.multiple_of(h * half, half), half)
            dz = mm_nt(g1[r].astype(BF16), rw[0])
            dpre[r, 0:chan] = (dz * fa0[r]).astype(BF16)
            dpre[r, chan:] = (dz * fb0[r]).astype(BF16)
            return 0

        lax.fori_loop(0, 2, part, 0)
        gr0 = mm_tn(z0[:, pl.ds(ymid, chan // 2)], g1[...].astype(BF16))
        if k == 0:
            accr[0] = gr0
        else:
            accr[0] = accr[0] + gr0

    def taps_back(lag):
        def at(r):
            return mm_nt(dpre[r], w0[lag * chan : (lag + 1) * chan])

        return at

    def over_halves(body):
        def part(h, _):
            body(pl.ds(pl.multiple_of(h * half, half), half))
            return 0

        lax.fori_loop(0, 2, part, 0)

    forward(0, s)
    out_copy = pltpu.make_async_copy(outv, out_ref.at[0], osem.at[0])
    out_copy.start()
    back_one(0, s)
    back_zero(0, s)
    transposed(s)
    for k in range(dp_count):
        q = (p + k) % dp_count
        acc0[k] = mm(lt[...], dpre[:, pl.ds(pl.multiple_of(q * col, col), col)])

    def direct(r):
        igv[r] = g1[r] + taps_back(0)(r)

    over_halves(direct)

    def lagged(r):
        hsend[r] = taps_back(1)(r).astype(BF16)

    @pl.when(c == 1)
    def _():
        over_halves(lagged)

    pl.when(y == 0)(take_over)
    forward(1, across)
    transposed(across)
    back_one(1, across)

    mine1, theirs1 = pl.multiple_of(c * own1, 128), pl.multiple_of((1 - c) * own1, 128)
    mine0, theirs0 = pl.multiple_of(c * own0, 128), pl.multiple_of((1 - c) * own0, 128)

    def pair_res(layer):
        return remote(csr.at[layer], crr.at[layer], cr_s.at[layer], cr_r.at[layer], {"seq": other})

    cs1[...] = acc1[pl.ds(theirs1, own1)].astype(BF16)
    pair1 = remote(cs1, cr1, c1_s, c1_r, {"seq": other})
    pair1.start()
    csr[1] = accr[1, pl.ds(theirs1, own1)].astype(BF16)
    pair_r1 = pair_res(1)
    pair_r1.start()

    back_zero(1, across)

    def spread(k, src, dst, send, recv):
        return remote(src, dst, send, recv, {"dp": (p + k) % dp_count})

    def send_res(layer):
        total = accr[layer, pl.ds(mine1, own1)] + crr[layer].astype(F32)
        accr[layer, pl.ds(mine1, own1)] = total
        copies = []
        for k in range(1, dp_count):
            q = (p + k) % dp_count
            part = accr[layer, pl.ds(mine1, own1), pl.ds(pl.multiple_of(q * rcol, rcol), rcol)]
            zsr[layer, k - 1] = part.astype(BF16)
            copy = spread(k, zsr.at[layer, k - 1], zrr.at[layer, k - 1], zc_s.at[layer, k - 1],
                          zc_r.at[layer, k - 1])
            copy.start()
            copies.append(copy)
        return copies

    pair1.wait_recv()
    acc1[pl.ds(mine1, own1)] = acc1[pl.ds(mine1, own1)] + cr1[...].astype(F32)
    over1 = []
    for k in range(1, dp_count):
        q = (p + k) % dp_count
        part = acc1[pl.ds(mine1, own1), pl.ds(pl.multiple_of(q * col, col), col)]
        zs1[k - 1] = part.astype(BF16)
        copy = spread(k, zs1.at[k - 1], zr1.at[k - 1], zb_s.at[k - 1], zb_r.at[k - 1])
        copy.start()
        over1.append(copy)
    pair_r1.wait_recv()
    over_r1 = send_res(1)

    csr[0] = accr[0, pl.ds(theirs1, own1)].astype(BF16)
    pair_r0 = pair_res(0)
    pair_r0.start()

    order = list(range(1, dp_count)) + [0]
    pairs0 = {}
    over0 = []

    def pass_on(k):
        pairs0[k].wait_recv()
        if k == 0:
            return
        zs0[k - 1] = (acc0[k, pl.ds(mine0, own0)] + cr0[k].astype(F32)).astype(BF16)
        copy = spread(k, zs0.at[k - 1], zr0.at[k - 1], za_s.at[k - 1], za_r.at[k - 1])
        copy.start()
        over0.append(copy)

    for place, k in enumerate(order):
        q = (p + k) % dp_count
        acc0[k] = acc0[k] + mm(lt[...], dpre[:, pl.ds(pl.multiple_of(q * col, col), col)])
        cs0[k] = acc0[k, pl.ds(theirs0, own0)].astype(BF16)
        pairs0[k] = remote(cs0.at[k], cr0.at[k], c0_s.at[k], c0_r.at[k], {"seq": other})
        pairs0[k].start()
        if place > 0:
            pass_on(order[place - 1])
    pair_r0.wait_recv()
    over_r0 = send_res(0)

    @pl.when(jnp.logical_and(c == 0, y == 0))
    def _():
        over_halves(lagged)

    pair_h = remote(hsend, hrecv, h_s, h_r, {"seq": other})
    pair_h.start()

    def lagged_twice(r):
        igv[r] = igv[r] + taps_back(2)(r)

    @pl.when(y == 0)
    def _():
        over_halves(lagged_twice)

    pass_on(0)
    pair_h.wait_recv()
    igv[...] = igv[...] + hrecv[...].astype(F32)
    ig_copy = pltpu.make_async_copy(igv, ig_ref.at[0], osem.at[1])
    ig_copy.start()

    for copy in over1:
        copy.wait_recv()
    here = pl.ds(pl.multiple_of(p * col, col), col)
    total1 = acc1[pl.ds(mine1, own1), here]
    for k in range(dp_count - 1):
        total1 = total1 + zr1[k].astype(F32)
    fs1[...] = total1

    to_first = remote(fs1, fr1.at[0], f_s, f_r.at[0], {"seq": 0})
    to_first2 = remote(fs1, fr1.at[1], f_s, f_r.at[1], {"seq": 0})
    to_second = remote(fs1, fr1.at[0], f_s, f_r.at[0], {"seq": 1})
    pl.when(s == 1)(to_first.start)
    pl.when(s == 2)(to_first2.start)
    pl.when(s == 3)(to_second.start)

    for layer, copies in ((1, over_r1), (0, over_r0)):
        for copy in copies:
            copy.wait_recv()
        total = accr[layer, pl.ds(mine1, own1), pl.ds(pl.multiple_of(p * rcol, rcol), rcol)]
        for k in range(dp_count - 1):
            total = total + zrr[layer, k].astype(F32)
        grv[layer] = total
    gr_copy = pltpu.make_async_copy(grv, gr_ref, osem.at[2])
    gr_copy.start()

    gcv[1] = jnp.zeros((own0, col), F32)

    @pl.when(s == 0)
    def _():
        gcv[1, 0:own1] = fs1[...]
        to_first.wait_recv()
        gcv[1, own1 : 2 * own1] = fr1[0]
        to_first2.wait_recv()
        gcv[1, 2 * own1 : 3 * own1] = fr1[1]

    @pl.when(s == 1)
    def _():
        to_second.wait_recv()
        gcv[1, 0:own1] = fr1[0]

    total0 = acc0[0, pl.ds(mine0, own0)] + cr0[0].astype(F32)
    for k in range(dp_count - 1):
        over0[k].wait_recv()
        total0 = total0 + zr0[k].astype(F32)
    gcv[0] = total0
    gc_copy = pltpu.make_async_copy(gcv, gc_ref, osem.at[3])
    gc_copy.start()

    for copy in s_over + c_over + [s_pair] + s_fwd + [pair1, pair_r1, pair_r0, pair_h]:
        copy.wait_send()
    for copy in list(pairs0.values()) + over1 + over_r1 + over_r0 + over0:
        copy.wait_send()
    pl.when(s > 0)(to_first.wait_send)
    for copy in (out_copy, ig_copy, gr_copy, gc_copy):
        copy.wait()


def fused(dp_count, stream_in, conv_weight, res_weight, out_cotangent):
    length, chan = stream_in.shape[1:]
    width, col, rcol = 2 * chan, 2 * chan // dp_count, chan // dp_count
    own0, own1 = 3 * chan // 4, chan // 4
    away = dp_count - 1
    v = pltpu.VMEM
    dma = pltpu.SemaphoreType.DMA
    return pl.pallas_call(
        functools.partial(fused_kernel, dp_count),
        out_shape=(
            jax.ShapeDtypeStruct((1, length, chan), BF16),
            jax.ShapeDtypeStruct((1, length, chan), F32),
            jax.ShapeDtypeStruct((2, own0, col), F32),
            jax.ShapeDtypeStruct((2, own1, rcol), F32),
        ),
        in_specs=[pl.BlockSpec(memory_space=pl.ANY)] * 4,
        out_specs=(pl.BlockSpec(memory_space=pl.ANY),) * 4,
        scratch_shapes=[
            v((6, length, chan), BF16), v((3 * chan, width), BF16), v((chan, width), BF16),
            v((2, chan, chan), BF16), v((2, length, chan), BF16),
            v((length, chan), F32), v((length, chan), F32), v((length, chan), F32),
            v((length, chan), F32), v((length, chan), BF16), v((length, chan), BF16),
            v((length, chan), BF16), v((length, width), BF16), v((length, chan), F32),
            v((3 * chan // 2, length), BF16),
            v((length, chan), BF16), v((length, chan), F32),
            v((length, chan), BF16), v((length, chan), BF16),
            v((dp_count, 2 * own0, col), F32), v((2 * own1, width), F32), v((2, 2 * own1, chan), F32),
            v((dp_count, own0, col), BF16), v((dp_count, own0, col), BF16),
            v((own1, width), BF16), v((own1, width), BF16),
            v((2, own1, chan), BF16), v((2, own1, chan), BF16),
            v((away, own0, col), BF16), v((away, own0, col), BF16),
            v((away, own1, col), BF16), v((away, own1, col), BF16),
            v((2, away, own1, rcol), BF16), v((2, away, own1, rcol), BF16),
            v((own1, col), F32), v((2, own1, col), F32),
            v((2, own0, col), F32), v((2, own1, rcol), F32),
            dma((5,)), dma((4,)), dma((2,)), dma((2,)), dma((2,)), dma((2,)), dma, dma,
            dma((2,)), dma((2,)), dma, dma,
            dma((dp_count,)), dma((dp_count,)), dma, dma, dma((2,)), dma((2,)),
            dma((away,)), dma((away,)), dma((away,)), dma((away,)),
            dma((2, away)), dma((2, away)), dma, dma((2,)),
        ],
        compiler_params=pltpu.CompilerParams(
            collective_id=0, has_side_effects=True, vmem_limit_bytes=50 * 1024 * 1024
        ),
        cost_estimate=pl.CostEstimate(flops=14 * 10**9, bytes_accessed=12 * 10**6, transcendentals=4 * 10**6),
    )(stream_in, conv_weight, res_weight, out_cotangent)


def dispatch(seq_count, dp_count, stream_in, conv_weight, res_weight, out_cotangent):
    records, length, channels = stream_in.shape
    fits = (
        seq_count == 4
        and dp_count == 4
        and records == 1
        and length == DILATION
        and channels == 512
        and conv_weight.shape[0] == 2
    )
    if fits:
        return fused(dp_count, stream_in, conv_weight, res_weight, out_cotangent)
    return local(stream_in, conv_weight, res_weight, out_cotangent)


def solution(mesh):
    placed = (P(("groups", "dp"), "seq", None), P(), P(), P(("groups", "dp"), "seq", None))
    return jax.shard_map(
        functools.partial(dispatch, mesh.shape["seq"], mesh.shape["dp"]),
        mesh=mesh,
        in_specs=placed,
        out_specs=(
            P(("groups", "dp"), "seq", None),
            P(("groups", "dp"), "seq", None),
            P("groups", "seq", "dp"),
            P("groups", "seq", "dp"),
        ),
        check_vma=False,
    )
```

```python
import functools

import jax
import jax.numpy as jnp
from jax import lax
from jax.experimental import pallas as pl
from jax.experimental.pallas import tpu as pltpu
from jax.sharding import PartitionSpec as P

DILATION = 512


def shifted(value, axis, steps):
    count = lax.axis_size(axis)
    leading, last = (max(0, -steps), min(count, count - steps))
    return lax.ppermute(value, axis, [(source, source + steps) for source in range(leading, last)])


def moved_back(values, distance):
    if distance >= lax.axis_size("seq"):
        return jnp.zeros_like(values)
    return shifted(values, "seq", distance)


def moved_ahead(values, distance):
    if distance >= lax.axis_size("seq"):
        return jnp.zeros_like(values)
    return shifted(values, "seq", -distance)


def looking_back(values, offset):
    length = values.shape[1]
    whole_shards, remainder = divmod(offset, length)
    return moved_back(values, whole_shards)


def looking_ahead(values, offset):
    length = values.shape[1]
    whole_shards, remainder = divmod(offset, length)
    return moved_ahead(values, whole_shards)


def spread_sum(left_side, right_side):
    contract = (((0,), (0,)), ((), ()))
    partial_value = lax.psum_scatter(
        lax.dot_general(left_side, right_side, contract, preferred_element_type=jnp.float32),
        "seq",
        scatter_dimension=0,
        tiled=True,
    )
    return lax.psum_scatter(partial_value, "dp", scatter_dimension=1, tiled=True)


def local(stream_in, conv_weight, res_weight, out_cotangent):
    records, length, channels = stream_in.shape
    layer_count = conv_weight.shape[0]
    stream = stream_in
    stored = []
    for layer_index in range(layer_count):
        spacing = DILATION * 4**layer_index
        taps = jnp.concatenate(
            [stream, looking_back(stream, spacing), looking_back(stream, 2 * spacing)], axis=2
        )
        taps_flat = taps.reshape(records * length, 3 * channels)
        preact = jnp.dot(taps_flat, conv_weight[layer_index], preferred_element_type=jnp.float32)
        filter_value = jnp.tanh(preact[:, :channels])
        gate_value = jax.nn.sigmoid(preact[:, channels:])
        gated = (filter_value * gate_value).astype(jnp.bfloat16)
        update = jnp.dot(gated, res_weight[layer_index], preferred_element_type=jnp.float32)
        stream = (
            (stream.reshape(-1, channels).astype(jnp.float32) + update)
            .astype(jnp.bfloat16)
            .reshape(records, length, channels)
        )
        stored.append((taps_flat, filter_value, gate_value, gated))
    stream_grad = out_cotangent.astype(jnp.float32).reshape(-1, channels)
    transpose_rhs = (((1,), (1,)), ((), ()))
    conv_grads = [None] * layer_count
    res_grads = [None] * layer_count
    for layer_index in reversed(range(layer_count)):
        spacing = DILATION * 4**layer_index
        taps_flat, filter_value, gate_value, gated = stored[layer_index]
        signal = stream_grad.astype(jnp.bfloat16)
        res_grads[layer_index] = spread_sum(gated, signal)
        gated_grad = lax.dot_general(
            signal, res_weight[layer_index], transpose_rhs, preferred_element_type=jnp.float32
        )
        filter_grad = gated_grad * gate_value * (1.0 - filter_value * filter_value)
        gate_grad = gated_grad * filter_value * gate_value * (1.0 - gate_value)
        pre_grad = jnp.concatenate([filter_grad, gate_grad], axis=1).astype(jnp.bfloat16)
        conv_grads[layer_index] = spread_sum(taps_flat, pre_grad)
        tap_grads = lax.dot_general(
            pre_grad, conv_weight[layer_index], transpose_rhs, preferred_element_type=jnp.float32
        ).astype(jnp.bfloat16)
        tap_grads = tap_grads.reshape(records, length, 3 * channels)
        first = tap_grads[:, :, :channels].astype(jnp.float32)
        second = looking_ahead(tap_grads[:, :, channels : 2 * channels], spacing).astype(
            jnp.float32
        )
        third = looking_ahead(tap_grads[:, :, 2 * channels :], 2 * spacing).astype(jnp.float32)
        stream_grad = stream_grad + (first + second + third).reshape(-1, channels)
    input_grad = stream_grad.reshape(records, length, channels)
    return (stream, input_grad, jnp.stack(conv_grads), jnp.stack(res_grads))


BF16 = jnp.bfloat16
F32 = jnp.float32
MESH = pl.DeviceIdType.MESH


def mm(left, right):
    return jnp.dot(left, right, preferred_element_type=F32)


def mm_nt(left, right):
    return lax.dot_general(left, right, (((1,), (1,)), ((), ())), preferred_element_type=F32)


def mm_tn(left, right):
    return lax.dot_general(left, right, (((0,), (0,)), ((), ())), preferred_element_type=F32)


def fused_kernel(
    dp_count,
    x_ref, w_ref, r_ref, ct_ref,
    out_ref, ig_ref, gcv, grv,
    sbuf, w0, w1, rw, ctb,
    fa0, fb0, fa1, fb1, z0, z1, s1, dpre, g1, lt,
    hsend, hrecv,
    acc0, acc1, accr,
    cs0, cr0, cs1, cr1, csr, crr,
    zs0, zr0, zs1, zr1, zsr, zrr, rel0, rel1, relr, pre_buf,
    fs1, fr1,
    lsem, ys_s, ys_r, yc_s, yc_r, xs_s, xs_r, fw_s, fw_r, h_s, h_r,
    c0_s, c0_r, c1_s, c1_r, cr_s, cr_r,
    za_s, za_r, zb_s, zb_r, zc_s, zc_r, f_s, f_r, ra_r, rb_r, rc_r,
):
    s = lax.axis_index("seq")
    p = lax.axis_index("dp")
    y = s // 2
    outv, igv = out_ref.at[0], ig_ref.at[0]
    c = s % 2
    other = s + 1 - 2 * c
    across = s + 2 - 4 * y
    length, chan = x_ref.shape[1], x_ref.shape[2]
    half = length // 2
    width = 2 * chan
    col = width // dp_count
    rcol = chan // dp_count
    own0 = 3 * chan // 4
    own1 = chan // 4
    ymid = pl.multiple_of(y * (chan // 2), 256)
    edge = jnp.logical_or(p == 0, p == dp_count - 1)
    near = jnp.where(p < 2, 3, 1)
    hops = [near, 4 - near, 2, 0]
    dest = [(p + hop) % dp_count for hop in hops]

    local_copies = [
        pltpu.make_async_copy(x_ref.at[0], sbuf.at[2 + s], lsem.at[0]),
        pltpu.make_async_copy(w_ref.at[0], w0, lsem.at[1]),
        pltpu.make_async_copy(r_ref, rw, lsem.at[2]),
        pltpu.make_async_copy(w_ref.at[1, pl.ds(0, chan)], w1, lsem.at[3]),
        pltpu.make_async_copy(ct_ref.at[0], ctb.at[0], lsem.at[4]),
    ]
    for copy in local_copies:
        copy.start()

    barrier = pltpu.get_barrier_semaphore()
    peers = [{"seq": other}, {"seq": across}]
    peers += [{"dp": (p + k) % dp_count} for k in range(1, dp_count)]
    for peer in peers:
        pl.semaphore_signal(barrier, inc=1, device_id=peer, device_id_type=MESH)
    pl.semaphore_wait(barrier, len(peers))

    def remote(src, dst, send, recv, device):
        return pltpu.make_async_remote_copy(
            src_ref=src, dst_ref=dst, send_sem=send, recv_sem=recv,
            device_id=device, device_id_type=MESH,
        )

    def rows(h):
        return pl.ds(h * half, half)

    s_over = [
        remote(x_ref.at[0, rows(h)], sbuf.at[2 + s, rows(h)], ys_s.at[h], ys_r.at[h], {"seq": across})
        for h in range(2)
    ]
    c_over = [
        remote(ct_ref.at[0, rows(h)], ctb.at[1, rows(h)], yc_s.at[h], yc_r.at[h], {"seq": across})
        for h in range(2)
    ]
    s_pair = remote(x_ref.at[0], sbuf.at[2 + s], xs_s, xs_r, {"seq": other})
    s_fwd = [
        remote(sbuf.at[2 + across, rows(h)], sbuf.at[2 + across, rows(h)], fw_s.at[h], fw_r.at[h],
               {"seq": other})
        for h in range(2)
    ]
    for h in range(2):
        s_over[h].start()
    s_pair.start()
    for h in range(2):
        c_over[h].start()

    sbuf[pl.ds(0, 2)] = jnp.zeros((2, length, chan), BF16)

    @pl.when(c == 0)
    def _():
        hsend[...] = jnp.zeros_like(hsend)

    for copy in local_copies:
        copy.wait()
    s_pair.wait_recv()

    def take_over(h):
        r = pl.ds(pl.multiple_of(h * half, half), half)
        remote(x_ref.at[0, r], sbuf.at[2 + across, r], ys_s.at[h], ys_r.at[h], {"seq": across}).wait_recv()
        forwarded = remote(sbuf.at[2 + across, r], sbuf.at[2 + across, r], fw_s.at[h], fw_r.at[h],
                           {"seq": other})
        forwarded.start()
        forwarded.wait_recv()

    def forward(k, u):
        def part(h, _):
            r = pl.ds(pl.multiple_of(h * half, half), half)
            if k == 1:
                pl.when(y == 0)(lambda: take_over(h))
            now = sbuf[u + 2, r]
            pre_buf[...] = mm(now, w0[0:chan])
            if k == 0:
                pl.when(y == 1)(lambda: take_over(h))

            @pl.when(u >= 1)
            def _():
                pre_buf[...] = pre_buf[...] + mm(sbuf[u + 1, r], w0[chan : 2 * chan])

            @pl.when(u >= 2)
            def _():
                pre_buf[...] = pre_buf[...] + mm(sbuf[u, r], w0[2 * chan :])

            def gate(filt, sig, fa, fb):
                f = jnp.tanh(filt)
                g = 0.5 * jnp.tanh(0.5 * sig) + 0.5
                fa[r] = g * (1.0 - f * f)
                fg = f * g
                fb[r] = fg * (1.0 - g)
                return fg.astype(BF16)

            z = gate(pre_buf[:, 0:chan], pre_buf[:, chan:], fa0, fb0)
            z0[r] = z
            nxt = (now.astype(F32) + mm(z, rw[0])).astype(BF16)
            s1[r] = nxt
            z = gate(mm(nxt, w1[:, 0:chan]), mm(nxt, w1[:, chan:]), fa1, fb1)
            z1[r] = z
            if k == 0:
                outv[r] = (nxt.astype(F32) + mm(z, rw[1])).astype(BF16)
            return 0

        lax.fori_loop(0, 2, part, 0)

    def transposed(k, u):
        def big():
            lt[pl.ds(ymid, chan)] = sbuf[u + 2 * (1 - y)].T

        if k == 0:
            big()
        else:
            pl.when(y == 0)(big)
        small = sbuf[u + 1, :, pl.ds(ymid, chan // 2)]
        lt[pl.ds(pl.multiple_of((1 - y) * chan, 256), chan // 2)] = small.T

    def back_one(k, u):
        def part(h, _):
            r = pl.ds(pl.multiple_of(h * half, half), half)
            if k == 1:
                for hh in range(2):
                    @pl.when(h == hh)
                    def _():
                        c_over[hh].wait_recv()
            e = ctb[k, r]
            dz = mm_nt(e, rw[1])
            df = (dz * fa1[r]).astype(BF16)
            dg = (dz * fb1[r]).astype(BF16)
            dpre[r, 0:chan] = df
            dpre[r, chan:] = dg
            g1[r] = e.astype(F32) + mm_nt(df, w1[:, 0:chan]) + mm_nt(dg, w1[:, chan:])
            return 0

        lax.fori_loop(0, 2, part, 0)
        gr1 = mm_tn(z1[:, pl.ds(ymid, chan // 2)], ctb[k])
        gc1 = mm_tn(s1[:, pl.ds(ymid, chan // 2)], dpre[...])
        if k == 0:
            accr[1] = gr1
            acc1[...] = gc1
        else:
            accr[1] = accr[1] + gr1
            acc1[...] = acc1[...] + gc1

    def back_zero(k, u):
        def part(h, _):
            r = pl.ds(pl.multiple_of(h * half, half), half)
            dz = mm_nt(g1[r].astype(BF16), rw[0])
            dpre[r, 0:chan] = (dz * fa0[r]).astype(BF16)
            dpre[r, chan:] = (dz * fb0[r]).astype(BF16)
            return 0

        if k == 0:
            lax.fori_loop(0, 2, part, 0)
        else:
            @pl.when(s != 2)
            def _():
                lax.fori_loop(0, 2, part, 0)
        gr0 = mm_tn(z0[:, pl.ds(ymid, chan // 2)], g1[...].astype(BF16))
        if k == 0:
            accr[0] = gr0
        else:
            accr[0] = accr[0] + gr0

    def taps_back(lag):
        def at(r):
            return mm_nt(dpre[r], w0[lag * chan : (lag + 1) * chan])

        return at

    def over_halves(body):
        def part(h, _):
            body(pl.ds(pl.multiple_of(h * half, half), half))
            return 0

        lax.fori_loop(0, 2, part, 0)

    forward(0, s)
    back_one(0, s)
    back_zero(0, s)
    transposed(0, s)
    for j in range(dp_count):
        acc0[j] = mm(lt[...], dpre[:, pl.ds(pl.multiple_of(dest[j] * col, 128), col)])

    def direct(r):
        igv[r] = g1[r] + taps_back(0)(r)

    over_halves(direct)

    def lagged(r):
        hsend[r] = taps_back(1)(r).astype(BF16)

    @pl.when(c == 1)
    def _():
        over_halves(lagged)

    forward(1, across)
    transposed(1, across)
    back_one(1, across)

    mine1, theirs1 = pl.multiple_of(c * own1, 128), pl.multiple_of((1 - c) * own1, 128)
    mine0, theirs0 = pl.multiple_of(c * own0, 128), pl.multiple_of((1 - c) * own0, 128)

    def pair_res(layer):
        return remote(csr.at[layer], crr.at[layer], cr_s.at[layer], cr_r.at[layer], {"seq": other})

    cs1[...] = acc1[pl.ds(theirs1, own1)].astype(BF16)
    pair1 = remote(cs1, cr1, c1_s, c1_r, {"seq": other})
    pair1.start()
    csr[1] = accr[1, pl.ds(theirs1, own1)].astype(BF16)
    pair_r1 = pair_res(1)
    pair_r1.start()

    back_zero(1, across)

    def along(j, src, dst, send, recv):
        slot = hops[j] - 1
        return remote(src.at[j], dst.at[slot], send.at[j], recv.at[slot], {"dp": dest[j]})

    def out_first(src, dst, relay, send, recv, relay_recv):
        direct = along(0, src, dst, send, recv)
        handed = remote(src.at[0], relay, send.at[0], relay_recv, {"dp": dest[1]})
        pl.when(jnp.logical_not(edge))(direct.start)
        pl.when(edge)(handed.start)
        return direct, handed

    def out_last(total, src, dst, relay, send, recv, handed):
        copy = along(2, src, dst, send, recv)

        @pl.when(edge)
        def _():
            src[2] = total.astype(BF16)

        @pl.when(jnp.logical_not(edge))
        def _():
            handed.wait_recv()
            src[2] = (total + relay[...].astype(F32)).astype(BF16)

        copy.start()
        return copy

    def gather_in(total, dst, home):
        home[...] = total + dst[1].astype(F32)

        @pl.when(p != 0)
        def _():
            home[...] = home[...] + dst[0].astype(F32)

        @pl.when(p != dp_count - 1)
        def _():
            home[...] = home[...] + dst[2].astype(F32)

    def arrived(src, dst, send, recv):
        def one(slot):
            return remote(src.at[0], dst.at[slot], send.at[0], recv.at[slot], {"dp": dest[1]})

        one(1).wait_recv()
        pl.when(p != 0)(one(0).wait_recv)
        pl.when(p != dp_count - 1)(one(2).wait_recv)

    def cols(j, size):
        return pl.ds(pl.multiple_of(dest[j] * size, 128), size)

    first = {}
    last = []
    m1 = pl.ds(mine1, own1)

    def start_one():
        pair1.wait_recv()
        acc1[m1] = acc1[m1] + cr1[...].astype(F32)
        for j in range(2):
            zs1[j] = acc1[m1, cols(j, col)].astype(BF16)
        first["1"] = out_first(zs1, zr1, rel1, zb_s, zb_r, rb_r)
        copy = along(1, zs1, zr1, zb_s, zb_r)
        copy.start()
        last.append(copy)

    def start_res(layer, pair):
        pair.wait_recv()
        accr[layer, m1] = accr[layer, m1] + crr[layer].astype(F32)
        for j in range(2):
            zsr[layer, j] = accr[layer, m1, cols(j, rcol)].astype(BF16)
        first[layer] = out_first(zsr.at[layer], zrr.at[layer], relr.at[layer], zc_s.at[layer],
                                 zc_r.at[layer], rc_r.at[layer])
        copy = along(1, zsr.at[layer], zrr.at[layer], zc_s.at[layer], zc_r.at[layer])
        copy.start()
        last.append(copy)

    def end_one():
        last.append(out_last(acc1[m1, cols(2, col)], zs1, zr1, rel1, zb_s, zb_r, first["1"][1]))

    def end_res(layer):
        last.append(out_last(accr[layer, m1, cols(2, rcol)], zsr.at[layer], zrr.at[layer],
                             relr.at[layer], zc_s.at[layer], zc_r.at[layer], first[layer][1]))

    start_one()
    start_res(1, pair_r1)

    csr[0] = accr[0, pl.ds(theirs1, own1)].astype(BF16)
    pair_r0 = pair_res(0)
    pair_r0.start()

    pairs0 = []
    m0 = pl.ds(mine0, own0)

    def pass_on(j):
        pairs0[j].wait_recv()
        total = acc0[j, m0] + cr0[j].astype(F32)
        if j < 2:
            zs0[j] = total.astype(BF16)
        if j == 0:
            first["0"] = out_first(zs0, zr0, rel0, za_s, za_r, ra_r)
        elif j == 1:
            copy = along(1, zs0, zr0, za_s, za_r)
            copy.start()
            last.append(copy)
        elif j == 2:
            last.append(out_last(total, zs0, zr0, rel0, za_s, za_r, first["0"][1]))

    for j in range(dp_count):
        @pl.when(y == 0)
        def _():
            acc0[j] = acc0[j] + mm(lt[...], dpre[:, cols(j, col)])

        @pl.when(s == 3)
        def _():
            small = pl.ds(0, chan // 2)
            acc0[j, small] = acc0[j, small] + mm(lt[small], dpre[:, cols(j, col)])

        cs0[j] = acc0[j, pl.ds(theirs0, own0)].astype(BF16)
        pairs0.append(remote(cs0.at[j], cr0.at[j], c0_s.at[j], c0_r.at[j], {"seq": other}))
        pairs0[j].start()
        if j == 1:
            pass_on(0)
            end_one()
            end_res(1)
        if j == 2:
            pass_on(1)
    start_res(0, pair_r0)

    @pl.when(jnp.logical_and(c == 0, y == 0))
    def _():
        over_halves(lagged)

    pair_h = remote(hsend, hrecv, h_s, h_r, {"seq": other})
    pair_h.start()

    def lagged_twice(r):
        igv[r] = igv[r] + taps_back(2)(r)

    @pl.when(y == 0)
    def _():
        over_halves(lagged_twice)

    pass_on(2)
    end_res(0)
    pass_on(3)
    pair_h.wait_recv()
    igv[...] = igv[...] + hrecv[...].astype(F32)

    arrived(zs1, zr1, zb_s, zb_r)
    gather_in(acc1[m1, cols(3, col)], zr1, fs1)

    to_first = remote(fs1, fr1.at[0], f_s, f_r.at[0], {"seq": 0})
    to_first2 = remote(fs1, fr1.at[1], f_s, f_r.at[1], {"seq": 0})
    to_second = remote(fs1, fr1.at[0], f_s, f_r.at[0], {"seq": 1})
    pl.when(s == 1)(to_first.start)
    pl.when(s == 2)(to_first2.start)
    pl.when(s == 3)(to_second.start)

    for layer in (1, 0):
        arrived(zsr.at[layer], zrr.at[layer], zc_s.at[layer], zc_r.at[layer])
        gather_in(accr[layer, m1, cols(3, rcol)], zrr.at[layer], grv.at[layer])

    gcv[1] = jnp.zeros((own0, col), F32)

    @pl.when(s == 0)
    def _():
        gcv[1, 0:own1] = fs1[...]
        to_first.wait_recv()
        gcv[1, own1 : 2 * own1] = fr1[0]
        to_first2.wait_recv()
        gcv[1, 2 * own1 : 3 * own1] = fr1[1]

    @pl.when(s == 1)
    def _():
        to_second.wait_recv()
        gcv[1, 0:own1] = fr1[0]

    arrived(zs0, zr0, za_s, za_r)
    gather_in(acc0[3, m0] + cr0[3].astype(F32), zr0, gcv.at[0])

    for copy in s_over + c_over + [s_pair] + s_fwd + [pair1, pair_r1, pair_r0, pair_h]:
        copy.wait_send()
    for copy in pairs0 + last + [direct for direct, handed in first.values()]:
        copy.wait_send()
    pl.when(s > 0)(to_first.wait_send)


def fused(dp_count, stream_in, conv_weight, res_weight, out_cotangent):
    length, chan = stream_in.shape[1:]
    width, col, rcol = 2 * chan, 2 * chan // dp_count, chan // dp_count
    own0, own1 = 3 * chan // 4, chan // 4
    away = dp_count - 1
    v = pltpu.VMEM
    dma = pltpu.SemaphoreType.DMA
    return pl.pallas_call(
        functools.partial(fused_kernel, dp_count),
        out_shape=(
            jax.ShapeDtypeStruct((1, length, chan), BF16),
            jax.ShapeDtypeStruct((1, length, chan), F32),
            jax.ShapeDtypeStruct((2, own0, col), F32),
            jax.ShapeDtypeStruct((2, own1, rcol), F32),
        ),
        in_specs=[pl.BlockSpec(memory_space=pltpu.HBM)] * 4,
        out_specs=(pl.BlockSpec(memory_space=pltpu.VMEM),) * 4,
        scratch_shapes=[
            v((6, length, chan), BF16), v((3 * chan, width), BF16), v((chan, width), BF16),
            v((2, chan, chan), BF16), v((2, length, chan), BF16),
            v((length, chan), F32), v((length, chan), F32), v((length, chan), F32),
            v((length, chan), F32), v((length, chan), BF16), v((length, chan), BF16),
            v((length, chan), BF16), v((length, width), BF16), v((length, chan), F32),
            v((3 * chan // 2, length), BF16),
            v((length, chan), BF16), v((length, chan), BF16),
            v((dp_count, 2 * own0, col), F32), v((2 * own1, width), F32), v((2, 2 * own1, chan), F32),
            v((dp_count, own0, col), BF16), v((dp_count, own0, col), BF16),
            v((own1, width), BF16), v((own1, width), BF16),
            v((2, own1, chan), BF16), v((2, own1, chan), BF16),
            v((away, own0, col), BF16), v((away, own0, col), BF16),
            v((away, own1, col), BF16), v((away, own1, col), BF16),
            v((2, away, own1, rcol), BF16), v((2, away, own1, rcol), BF16),
            v((own0, col), BF16), v((own1, col), BF16), v((2, own1, rcol), BF16),
            v((length // 2, width), F32),
            v((own1, col), F32), v((2, own1, col), F32),
            dma((5,)), dma((2,)), dma((2,)), dma((2,)), dma((2,)), dma, dma,
            dma((2,)), dma((2,)), dma, dma,
            dma((dp_count,)), dma((dp_count,)), dma, dma, dma((2,)), dma((2,)),
            dma((away,)), dma((away,)), dma((away,)), dma((away,)),
            dma((2, away)), dma((2, away)), dma, dma((2,)), dma, dma, dma((2,)),
        ],
        compiler_params=pltpu.CompilerParams(
            collective_id=0, has_side_effects=True, vmem_limit_bytes=50 * 1024 * 1024
        ),
        cost_estimate=pl.CostEstimate(flops=14 * 10**9, bytes_accessed=12 * 10**6, transcendentals=4 * 10**6),
    )(stream_in, conv_weight, res_weight, out_cotangent)


def dispatch(seq_count, dp_count, stream_in, conv_weight, res_weight, out_cotangent):
    records, length, channels = stream_in.shape
    fits = (
        seq_count == 4
        and dp_count == 4
        and records == 1
        and length == DILATION
        and channels == 512
        and conv_weight.shape[0] == 2
    )
    if fits:
        return fused(dp_count, stream_in, conv_weight, res_weight, out_cotangent)
    return local(stream_in, conv_weight, res_weight, out_cotangent)


def solution(mesh):
    placed = (P(("groups", "dp"), "seq", None), P(), P(), P(("groups", "dp"), "seq", None))
    return jax.shard_map(
        functools.partial(dispatch, mesh.shape["seq"], mesh.shape["dp"]),
        mesh=mesh,
        in_specs=placed,
        out_specs=(
            P(("groups", "dp"), "seq", None),
            P(("groups", "dp"), "seq", None),
            P("groups", "seq", "dp"),
            P("groups", "seq", "dp"),
        ),
        check_vma=False,
    )
```

```python
import functools

import jax
import jax.numpy as jnp
from jax import lax
from jax.experimental import pallas as pl
from jax.experimental.pallas import tpu as pltpu
from jax.sharding import PartitionSpec as P

DILATION = 512


def shifted(value, axis, steps):
    count = lax.axis_size(axis)
    leading, last = (max(0, -steps), min(count, count - steps))
    return lax.ppermute(value, axis, [(source, source + steps) for source in range(leading, last)])


def moved_back(values, distance):
    if distance >= lax.axis_size("seq"):
        return jnp.zeros_like(values)
    return shifted(values, "seq", distance)


def moved_ahead(values, distance):
    if distance >= lax.axis_size("seq"):
        return jnp.zeros_like(values)
    return shifted(values, "seq", -distance)


def looking_back(values, offset):
    length = values.shape[1]
    whole_shards, remainder = divmod(offset, length)
    return moved_back(values, whole_shards)


def looking_ahead(values, offset):
    length = values.shape[1]
    whole_shards, remainder = divmod(offset, length)
    return moved_ahead(values, whole_shards)


def spread_sum(left_side, right_side):
    contract = (((0,), (0,)), ((), ()))
    partial_value = lax.psum_scatter(
        lax.dot_general(left_side, right_side, contract, preferred_element_type=jnp.float32),
        "seq",
        scatter_dimension=0,
        tiled=True,
    )
    return lax.psum_scatter(partial_value, "dp", scatter_dimension=1, tiled=True)


def local(stream_in, conv_weight, res_weight, out_cotangent):
    records, length, channels = stream_in.shape
    layer_count = conv_weight.shape[0]
    stream = stream_in
    stored = []
    for layer_index in range(layer_count):
        spacing = DILATION * 4**layer_index
        taps = jnp.concatenate(
            [stream, looking_back(stream, spacing), looking_back(stream, 2 * spacing)], axis=2
        )
        taps_flat = taps.reshape(records * length, 3 * channels)
        preact = jnp.dot(taps_flat, conv_weight[layer_index], preferred_element_type=jnp.float32)
        filter_value = jnp.tanh(preact[:, :channels])
        gate_value = jax.nn.sigmoid(preact[:, channels:])
        gated = (filter_value * gate_value).astype(jnp.bfloat16)
        update = jnp.dot(gated, res_weight[layer_index], preferred_element_type=jnp.float32)
        stream = (
            (stream.reshape(-1, channels).astype(jnp.float32) + update)
            .astype(jnp.bfloat16)
            .reshape(records, length, channels)
        )
        stored.append((taps_flat, filter_value, gate_value, gated))
    stream_grad = out_cotangent.astype(jnp.float32).reshape(-1, channels)
    transpose_rhs = (((1,), (1,)), ((), ()))
    conv_grads = [None] * layer_count
    res_grads = [None] * layer_count
    for layer_index in reversed(range(layer_count)):
        spacing = DILATION * 4**layer_index
        taps_flat, filter_value, gate_value, gated = stored[layer_index]
        signal = stream_grad.astype(jnp.bfloat16)
        res_grads[layer_index] = spread_sum(gated, signal)
        gated_grad = lax.dot_general(
            signal, res_weight[layer_index], transpose_rhs, preferred_element_type=jnp.float32
        )
        filter_grad = gated_grad * gate_value * (1.0 - filter_value * filter_value)
        gate_grad = gated_grad * filter_value * gate_value * (1.0 - gate_value)
        pre_grad = jnp.concatenate([filter_grad, gate_grad], axis=1).astype(jnp.bfloat16)
        conv_grads[layer_index] = spread_sum(taps_flat, pre_grad)
        tap_grads = lax.dot_general(
            pre_grad, conv_weight[layer_index], transpose_rhs, preferred_element_type=jnp.float32
        ).astype(jnp.bfloat16)
        tap_grads = tap_grads.reshape(records, length, 3 * channels)
        first = tap_grads[:, :, :channels].astype(jnp.float32)
        second = looking_ahead(tap_grads[:, :, channels : 2 * channels], spacing).astype(
            jnp.float32
        )
        third = looking_ahead(tap_grads[:, :, 2 * channels :], 2 * spacing).astype(jnp.float32)
        stream_grad = stream_grad + (first + second + third).reshape(-1, channels)
    input_grad = stream_grad.reshape(records, length, channels)
    return (stream, input_grad, jnp.stack(conv_grads), jnp.stack(res_grads))


BF16 = jnp.bfloat16
F32 = jnp.float32
MESH = pl.DeviceIdType.MESH


def mm(left, right):
    return jnp.dot(left, right, preferred_element_type=F32)


def mm_nt(left, right):
    return lax.dot_general(left, right, (((1,), (1,)), ((), ())), preferred_element_type=F32)


def mm_tn(left, right):
    return lax.dot_general(left, right, (((0,), (0,)), ((), ())), preferred_element_type=F32)


def fused_kernel(
    dp_count,
    x_ref, w_ref, r_ref, ct_ref,
    out_ref, ig_ref, gcv, grv,
    sbuf, w0, w1, rw, ctb,
    fa0, fb0, fa1, fb1, z0, z1, s1, dpre, g1, lt,
    hsend, hrecv,
    acc0, acc1, accr,
    cs0, cr0, cs1, cr1, csr, crr,
    zs0, zr0, zs1, zr1, zsr, zrr, rel0, rel1, relr, pre_buf,
    fs1, fr1,
    lsem, ys_s, ys_r, yc_s, yc_r, xs_s, xs_r, fw_s, fw_r, h_s, h_r,
    c0_s, c0_r, c1_s, c1_r, cr_s, cr_r,
    za_s, za_r, zb_s, zb_r, zc_s, zc_r, f_s, f_r, ra_r, rb_r, rc_r,
):
    s = lax.axis_index("seq")
    p = lax.axis_index("dp")
    y = s // 2
    outv, igv = out_ref.at[0], ig_ref.at[0]
    c = s % 2
    other = s + 1 - 2 * c
    across = s + 2 - 4 * y
    length, chan = x_ref.shape[1], x_ref.shape[2]
    half = length // 2
    width = 2 * chan
    col = width // dp_count
    rcol = chan // dp_count
    own0 = 3 * chan // 4
    own1 = chan // 4
    ymid = pl.multiple_of(y * (chan // 2), 256)
    edge = jnp.logical_or(p == 0, p == dp_count - 1)
    near = jnp.where(p < 2, 3, 1)
    hops = [near, 4 - near, 2, 0]
    dest = [(p + hop) % dp_count for hop in hops]

    local_copies = [
        pltpu.make_async_copy(x_ref.at[0], sbuf.at[2 + s], lsem.at[0]),
        pltpu.make_async_copy(w_ref.at[0], w0, lsem.at[1]),
        pltpu.make_async_copy(r_ref, rw, lsem.at[2]),
        pltpu.make_async_copy(w_ref.at[1, pl.ds(0, chan)], w1, lsem.at[3]),
        pltpu.make_async_copy(ct_ref.at[0], ctb.at[0], lsem.at[4]),
    ]
    for copy in local_copies:
        copy.start()

    barrier = pltpu.get_barrier_semaphore()
    peers = [{"seq": other}, {"seq": across}]
    peers += [{"dp": (p + k) % dp_count} for k in range(1, dp_count)]
    for peer in peers:
        pl.semaphore_signal(barrier, inc=1, device_id=peer, device_id_type=MESH)
    pl.semaphore_wait(barrier, len(peers))

    def remote(src, dst, send, recv, device):
        return pltpu.make_async_remote_copy(
            src_ref=src, dst_ref=dst, send_sem=send, recv_sem=recv,
            device_id=device, device_id_type=MESH,
        )

    def rows(h):
        return pl.ds(h * half, half)

    s_over = [
        remote(x_ref.at[0, rows(h)], sbuf.at[2 + s, rows(h)], ys_s.at[h], ys_r.at[h], {"seq": across})
        for h in range(2)
    ]
    c_over = [
        remote(ct_ref.at[0, rows(h)], ctb.at[1, rows(h)], yc_s.at[h], yc_r.at[h], {"seq": across})
        for h in range(2)
    ]
    s_pair = remote(x_ref.at[0], sbuf.at[2 + s], xs_s, xs_r, {"seq": other})
    s_fwd = [
        remote(sbuf.at[2 + across, rows(h)], sbuf.at[2 + across, rows(h)], fw_s.at[h], fw_r.at[h],
               {"seq": other})
        for h in range(2)
    ]
    for h in range(2):
        s_over[h].start()
    s_pair.start()
    for h in range(2):
        c_over[h].start()

    sbuf[pl.ds(0, 2)] = jnp.zeros((2, length, chan), BF16)

    @pl.when(c == 0)
    def _():
        hsend[...] = jnp.zeros_like(hsend)

    for copy in local_copies:
        copy.wait()
    s_pair.wait_recv()

    def take_over(h):
        r = pl.ds(pl.multiple_of(h * half, half), half)
        remote(x_ref.at[0, r], sbuf.at[2 + across, r], ys_s.at[h], ys_r.at[h], {"seq": across}).wait_recv()
        forwarded = remote(sbuf.at[2 + across, r], sbuf.at[2 + across, r], fw_s.at[h], fw_r.at[h],
                           {"seq": other})
        forwarded.start()
        forwarded.wait_recv()

    def forward(k, u):
        def part(h, _):
            r = pl.ds(pl.multiple_of(h * half, half), half)
            if k == 1:
                pl.when(y == 0)(lambda: take_over(h))
            now = sbuf[u + 2, r]
            pre_buf[...] = mm(now, w0[0:chan])
            if k == 0:
                pl.when(y == 1)(lambda: take_over(h))

            @pl.when(u >= 1)
            def _():
                pre_buf[...] = pre_buf[...] + mm(sbuf[u + 1, r], w0[chan : 2 * chan])

            @pl.when(u >= 2)
            def _():
                pre_buf[...] = pre_buf[...] + mm(sbuf[u, r], w0[2 * chan :])

            def gate(filt, sig, fa, fb):
                f = jnp.tanh(filt)
                g = 0.5 * jnp.tanh(0.5 * sig) + 0.5
                fa[r] = g * (1.0 - f * f)
                fg = f * g
                fb[r] = fg * (1.0 - g)
                return fg.astype(BF16)

            z = gate(pre_buf[:, 0:chan], pre_buf[:, chan:], fa0, fb0)
            z0[r] = z
            nxt = (now.astype(F32) + mm(z, rw[0])).astype(BF16)
            s1[r] = nxt
            z = gate(mm(nxt, w1[:, 0:chan]), mm(nxt, w1[:, chan:]), fa1, fb1)
            z1[r] = z
            if k == 0:
                outv[r] = (nxt.astype(F32) + mm(z, rw[1])).astype(BF16)
            return 0

        lax.fori_loop(0, 2, part, 0)

    def transposed(k, u):
        def big():
            lt[pl.ds(ymid, chan)] = sbuf[u + 2 * (1 - y)].T

        if k == 0:
            big()
        else:
            pl.when(y == 0)(big)
        small = sbuf[u + 1, :, pl.ds(ymid, chan // 2)]
        lt[pl.ds(pl.multiple_of((1 - y) * chan, 256), chan // 2)] = small.T

    def back_one(k, u):
        def part(h, _):
            r = pl.ds(pl.multiple_of(h * half, half), half)
            if k == 1:
                for hh in range(2):
                    @pl.when(h == hh)
                    def _():
                        c_over[hh].wait_recv()
            e = ctb[k, r]
            dz = mm_nt(e, rw[1])
            df = (dz * fa1[r]).astype(BF16)
            dg = (dz * fb1[r]).astype(BF16)
            dpre[r, 0:chan] = df
            dpre[r, chan:] = dg
            g1[r] = e.astype(F32) + mm_nt(df, w1[:, 0:chan]) + mm_nt(dg, w1[:, chan:])
            return 0

        lax.fori_loop(0, 2, part, 0)
        gr1 = mm_tn(z1[:, pl.ds(ymid, chan // 2)], ctb[k])
        gc1 = mm_tn(s1[:, pl.ds(ymid, chan // 2)], dpre[...])
        if k == 0:
            accr[1] = gr1
            acc1[...] = gc1
        else:
            accr[1] = accr[1] + gr1
            acc1[...] = acc1[...] + gc1

    def back_zero(k, u, between=None):
        def part(h, _):
            r = pl.ds(pl.multiple_of(h * half, half), half)
            dz = mm_nt(g1[r].astype(BF16), rw[0])
            dpre[r, 0:chan] = (dz * fa0[r]).astype(BF16)
            dpre[r, chan:] = (dz * fb0[r]).astype(BF16)
            return 0

        if k == 0:
            lax.fori_loop(0, 2, part, 0)
        else:
            for h in range(2):
                @pl.when(s != 2)
                def _():
                    lax.fori_loop(h, h + 1, part, 0)

                between[h]()
        gr0 = mm_tn(z0[:, pl.ds(ymid, chan // 2)], g1[...].astype(BF16))
        if k == 0:
            accr[0] = gr0
        else:
            accr[0] = accr[0] + gr0

    def taps_back(lag):
        def at(r):
            return mm_nt(dpre[r], w0[lag * chan : (lag + 1) * chan])

        return at

    def over_halves(body):
        def part(h, _):
            body(pl.ds(pl.multiple_of(h * half, half), half))
            return 0

        lax.fori_loop(0, 2, part, 0)

    forward(0, s)
    back_one(0, s)
    back_zero(0, s)
    transposed(0, s)
    for j in range(dp_count):
        acc0[j] = mm(lt[...], dpre[:, pl.ds(pl.multiple_of(dest[j] * col, 128), col)])

    def direct(r):
        igv[r] = g1[r] + taps_back(0)(r)

    over_halves(direct)

    def lagged(r):
        hsend[r] = taps_back(1)(r).astype(BF16)

    @pl.when(c == 1)
    def _():
        over_halves(lagged)

    forward(1, across)
    transposed(1, across)
    back_one(1, across)

    mine1, theirs1 = pl.multiple_of(c * own1, 128), pl.multiple_of((1 - c) * own1, 128)
    mine0, theirs0 = pl.multiple_of(c * own0, 128), pl.multiple_of((1 - c) * own0, 128)

    def pair_res(layer):
        return remote(csr.at[layer], crr.at[layer], cr_s.at[layer], cr_r.at[layer], {"seq": other})

    cs1[...] = acc1[pl.ds(theirs1, own1)].astype(BF16)
    pair1 = remote(cs1, cr1, c1_s, c1_r, {"seq": other})
    pair1.start()
    csr[1] = accr[1, pl.ds(theirs1, own1)].astype(BF16)
    pair_r1 = pair_res(1)
    pair_r1.start()


    def along(j, src, dst, send, recv):
        slot = hops[j] - 1
        return remote(src.at[j], dst.at[slot], send.at[j], recv.at[slot], {"dp": dest[j]})

    def out_first(src, dst, relay, send, recv, relay_recv):
        direct = along(0, src, dst, send, recv)
        handed = remote(src.at[0], relay, send.at[0], relay_recv, {"dp": dest[1]})
        pl.when(jnp.logical_not(edge))(direct.start)
        pl.when(edge)(handed.start)
        return direct, handed

    def out_last(total, src, dst, relay, send, recv, handed):
        copy = along(2, src, dst, send, recv)

        @pl.when(edge)
        def _():
            src[2] = total.astype(BF16)

        @pl.when(jnp.logical_not(edge))
        def _():
            handed.wait_recv()
            src[2] = (total + relay[...].astype(F32)).astype(BF16)

        copy.start()
        return copy

    def gather_in(total, dst, home):
        home[...] = total + dst[1].astype(F32)

        @pl.when(p != 0)
        def _():
            home[...] = home[...] + dst[0].astype(F32)

        @pl.when(p != dp_count - 1)
        def _():
            home[...] = home[...] + dst[2].astype(F32)

    def arrived(src, dst, send, recv):
        def one(slot):
            return remote(src.at[0], dst.at[slot], send.at[0], recv.at[slot], {"dp": dest[1]})

        one(1).wait_recv()
        pl.when(p != 0)(one(0).wait_recv)
        pl.when(p != dp_count - 1)(one(2).wait_recv)

    def cols(j, size):
        return pl.ds(pl.multiple_of(dest[j] * size, 128), size)

    first = {}
    last = []
    m1 = pl.ds(mine1, own1)

    def start_one():
        pair1.wait_recv()
        acc1[m1] = acc1[m1] + cr1[...].astype(F32)
        for j in range(2):
            zs1[j] = acc1[m1, cols(j, col)].astype(BF16)
        first["1"] = out_first(zs1, zr1, rel1, zb_s, zb_r, rb_r)
        copy = along(1, zs1, zr1, zb_s, zb_r)
        copy.start()
        last.append(copy)

    def start_res(layer, pair):
        pair.wait_recv()
        accr[layer, m1] = accr[layer, m1] + crr[layer].astype(F32)
        for j in range(2):
            zsr[layer, j] = accr[layer, m1, cols(j, rcol)].astype(BF16)
        first[layer] = out_first(zsr.at[layer], zrr.at[layer], relr.at[layer], zc_s.at[layer],
                                 zc_r.at[layer], rc_r.at[layer])
        copy = along(1, zsr.at[layer], zrr.at[layer], zc_s.at[layer], zc_r.at[layer])
        copy.start()
        last.append(copy)

    def end_one():
        last.append(out_last(acc1[m1, cols(2, col)], zs1, zr1, rel1, zb_s, zb_r, first["1"][1]))

    def end_res(layer):
        last.append(out_last(accr[layer, m1, cols(2, rcol)], zsr.at[layer], zrr.at[layer],
                             relr.at[layer], zc_s.at[layer], zc_r.at[layer], first[layer][1]))

    back_zero(1, across, (start_one, lambda: start_res(1, pair_r1)))

    csr[0] = accr[0, pl.ds(theirs1, own1)].astype(BF16)
    pair_r0 = pair_res(0)
    pair_r0.start()

    pairs0 = []
    m0 = pl.ds(mine0, own0)

    def pass_on(j):
        pairs0[j].wait_recv()
        total = acc0[j, m0] + cr0[j].astype(F32)
        if j < 2:
            zs0[j] = total.astype(BF16)
        if j == 0:
            first["0"] = out_first(zs0, zr0, rel0, za_s, za_r, ra_r)
        elif j == 1:
            copy = along(1, zs0, zr0, za_s, za_r)
            copy.start()
            last.append(copy)
        elif j == 2:
            last.append(out_last(total, zs0, zr0, rel0, za_s, za_r, first["0"][1]))

    for j in range(dp_count):
        @pl.when(y == 0)
        def _():
            acc0[j] = acc0[j] + mm(lt[...], dpre[:, cols(j, col)])

        @pl.when(s == 3)
        def _():
            small = pl.ds(0, chan // 2)
            acc0[j, small] = acc0[j, small] + mm(lt[small], dpre[:, cols(j, col)])

        cs0[j] = acc0[j, pl.ds(theirs0, own0)].astype(BF16)
        pairs0.append(remote(cs0.at[j], cr0.at[j], c0_s.at[j], c0_r.at[j], {"seq": other}))
        pairs0[j].start()
        if j == 1:
            pass_on(0)
            end_one()
            end_res(1)
        if j == 2:
            pass_on(1)
    start_res(0, pair_r0)

    @pl.when(jnp.logical_and(c == 0, y == 0))
    def _():
        over_halves(lagged)

    pair_h = remote(hsend, hrecv, h_s, h_r, {"seq": other})
    pair_h.start()

    pass_on(2)
    end_res(0)

    def lagged_twice(r):
        igv[r] = igv[r] + taps_back(2)(r)

    @pl.when(y == 0)
    def _():
        over_halves(lagged_twice)

    pass_on(3)
    pair_h.wait_recv()
    igv[...] = igv[...] + hrecv[...].astype(F32)

    arrived(zs1, zr1, zb_s, zb_r)
    gather_in(acc1[m1, cols(3, col)], zr1, fs1)

    to_first = remote(fs1, fr1.at[0], f_s, f_r.at[0], {"seq": 0})
    to_first2 = remote(fs1, fr1.at[1], f_s, f_r.at[1], {"seq": 0})
    to_second = remote(fs1, fr1.at[0], f_s, f_r.at[0], {"seq": 1})
    pl.when(s == 1)(to_first.start)
    pl.when(s == 2)(to_first2.start)
    pl.when(s == 3)(to_second.start)

    for layer in (1, 0):
        arrived(zsr.at[layer], zrr.at[layer], zc_s.at[layer], zc_r.at[layer])
        gather_in(accr[layer, m1, cols(3, rcol)], zrr.at[layer], grv.at[layer])

    gcv[1] = jnp.zeros((own0, col), F32)

    @pl.when(s == 0)
    def _():
        gcv[1, 0:own1] = fs1[...]
        to_first.wait_recv()
        gcv[1, own1 : 2 * own1] = fr1[0]
        to_first2.wait_recv()
        gcv[1, 2 * own1 : 3 * own1] = fr1[1]

    @pl.when(s == 1)
    def _():
        to_second.wait_recv()
        gcv[1, 0:own1] = fr1[0]

    arrived(zs0, zr0, za_s, za_r)
    gather_in(acc0[3, m0] + cr0[3].astype(F32), zr0, gcv.at[0])

    for copy in s_over + c_over + [s_pair] + s_fwd + [pair1, pair_r1, pair_r0, pair_h]:
        copy.wait_send()
    for copy in pairs0 + last + [direct for direct, handed in first.values()]:
        copy.wait_send()
    pl.when(s > 0)(to_first.wait_send)


def fused(dp_count, stream_in, conv_weight, res_weight, out_cotangent):
    length, chan = stream_in.shape[1:]
    width, col, rcol = 2 * chan, 2 * chan // dp_count, chan // dp_count
    own0, own1 = 3 * chan // 4, chan // 4
    away = dp_count - 1
    v = pltpu.VMEM
    dma = pltpu.SemaphoreType.DMA
    return pl.pallas_call(
        functools.partial(fused_kernel, dp_count),
        out_shape=(
            jax.ShapeDtypeStruct((1, length, chan), BF16),
            jax.ShapeDtypeStruct((1, length, chan), F32),
            jax.ShapeDtypeStruct((2, own0, col), F32),
            jax.ShapeDtypeStruct((2, own1, rcol), F32),
        ),
        in_specs=[pl.BlockSpec(memory_space=pltpu.HBM)] * 4,
        out_specs=(pl.BlockSpec(memory_space=pltpu.VMEM),) * 4,
        scratch_shapes=[
            v((6, length, chan), BF16), v((3 * chan, width), BF16), v((chan, width), BF16),
            v((2, chan, chan), BF16), v((2, length, chan), BF16),
            v((length, chan), F32), v((length, chan), F32), v((length, chan), F32),
            v((length, chan), F32), v((length, chan), BF16), v((length, chan), BF16),
            v((length, chan), BF16), v((length, width), BF16), v((length, chan), F32),
            v((3 * chan // 2, length), BF16),
            v((length, chan), BF16), v((length, chan), BF16),
            v((dp_count, 2 * own0, col), F32), v((2 * own1, width), F32), v((2, 2 * own1, chan), F32),
            v((dp_count, own0, col), BF16), v((dp_count, own0, col), BF16),
            v((own1, width), BF16), v((own1, width), BF16),
            v((2, own1, chan), BF16), v((2, own1, chan), BF16),
            v((away, own0, col), BF16), v((away, own0, col), BF16),
            v((away, own1, col), BF16), v((away, own1, col), BF16),
            v((2, away, own1, rcol), BF16), v((2, away, own1, rcol), BF16),
            v((own0, col), BF16), v((own1, col), BF16), v((2, own1, rcol), BF16),
            v((length // 2, width), F32),
            v((own1, col), F32), v((2, own1, col), F32),
            dma((5,)), dma((2,)), dma((2,)), dma((2,)), dma((2,)), dma, dma,
            dma((2,)), dma((2,)), dma, dma,
            dma((dp_count,)), dma((dp_count,)), dma, dma, dma((2,)), dma((2,)),
            dma((away,)), dma((away,)), dma((away,)), dma((away,)),
            dma((2, away)), dma((2, away)), dma, dma((2,)), dma, dma, dma((2,)),
        ],
        compiler_params=pltpu.CompilerParams(
            collective_id=0, has_side_effects=True, vmem_limit_bytes=50 * 1024 * 1024
        ),
        cost_estimate=pl.CostEstimate(flops=14 * 10**9, bytes_accessed=12 * 10**6, transcendentals=4 * 10**6),
    )(stream_in, conv_weight, res_weight, out_cotangent)


def dispatch(seq_count, dp_count, stream_in, conv_weight, res_weight, out_cotangent):
    records, length, channels = stream_in.shape
    fits = (
        seq_count == 4
        and dp_count == 4
        and records == 1
        and length == DILATION
        and channels == 512
        and conv_weight.shape[0] == 2
    )
    if fits:
        return fused(dp_count, stream_in, conv_weight, res_weight, out_cotangent)
    return local(stream_in, conv_weight, res_weight, out_cotangent)


def solution(mesh):
    placed = (P(("groups", "dp"), "seq", None), P(), P(), P(("groups", "dp"), "seq", None))
    return jax.shard_map(
        functools.partial(dispatch, mesh.shape["seq"], mesh.shape["dp"]),
        mesh=mesh,
        in_specs=placed,
        out_specs=(
            P(("groups", "dp"), "seq", None),
            P(("groups", "dp"), "seq", None),
            P("groups", "seq", "dp"),
            P("groups", "seq", "dp"),
        ),
        check_vma=False,
    )
```
